32 devices in a mesh: row: 4 (over z), col: 8 (over y, x, core).
Axes of the slice: x: 2, y: 2, z: 4, core: 2. Of those that a mesh axis runs over, the one named last changes fastest.
Arguments:
- lensed_picture_vectors: bfloat16 [6144, 512], P(('row', 'col')), may hold values from -6 to 6
- theta_feature_vectors: bfloat16 [6144, 512], P(('row', 'col')), may hold values from -6 to 6
- prior_domain_label: int32 [6144], P(('row', 'col')), may hold values from 0 to 63, as said below
- matched_theta_index: int32 [6144], P(('row', 'col')), may hold values from 0 to 6143, each once
- affinity_gain: float32 [1], replicated, may hold values from 5 to 15
- affinity_shift: float32 [1], replicated, may hold values from -4 to -1
Outputs:
- loss: float32 [1], replicated
- grad_data: float32 [6144, 512], P(('row', 'col'))
- grad_param: float32 [6144, 512], P(('row', 'col'))
The draws below stay inside these ranges and needn't reach their ends.
Inputs may be any that keep to these rules, and one draw needn't show every extreme that they name: `matched_theta_index`: a permutation of the pair indices. `prior_domain_label`: region 0 is shared by a share of the pairs that differs between blocks of 192 pairs.
All inputs are finite; a program needn't handle non-finite values.
Results may differ from the reference program's by a relative error of at most 0.00086.
Values may be sent and summed in bfloat16 or wider, within the bound.
No kernel may reach another device: no remote copies, remote signals or barrier semaphores. Data moves between devices by JAX's collectives and lax.ppermute only.
A program may use at most 64 MiB of HBM per device.

```python
import math
import jax
import jax.numpy as jnp
from jax import lax

E = 512
ROW_DEV = 192
REGIONS = 64
TOKENS = 6144
N_ROW = 4
N_COL = 8


def shared_part(key, salt):
    groups = TOKENS // ROW_DEV
    direction = jax.random.normal(jax.random.fold_in(key, 101), (E,), jnp.float32)
    key_sign, key_strength = jax.random.split(jax.random.fold_in(key, salt), 2)
    polarity = jnp.where(jax.random.bernoulli(key_sign, 0.5, (TOKENS, 1)), 1.0, -1.0).astype(jnp.float32)
    strength = jax.random.uniform(key_strength, (groups, 1), jnp.float32, 0.0, 2.5)
    strength = jnp.repeat(strength, ROW_DEV, axis=0)
    return strength * polarity * direction[None, :]


def draw_lensed_picture_vectors(key, part):
    key_noise = jax.random.fold_in(key, 211)
    noise = jax.random.normal(key_noise, (TOKENS, E), jnp.float32)
    values = noise + shared_part(key, 307)
    return jnp.clip(values, -6.0, 6.0).astype(jnp.bfloat16)


def draw_theta_feature_vectors(key, part):
    key_noise = jax.random.fold_in(key, 223)
    noise = jax.random.normal(key_noise, (TOKENS, E), jnp.float32)
    values = noise + shared_part(key, 311)
    return jnp.clip(values, -6.0, 6.0).astype(jnp.bfloat16)


def draw_prior_domain_label(key, part):
    groups = TOKENS // ROW_DEV
    key_base, key_spread, key_offset, key_share, key_common, key_factor = jax.random.split(jax.random.fold_in(key, 17), 6)
    common_base = jax.random.randint(key_common, (), 0, REGIONS - 1)
    shared_flag = jax.random.randint(key_share, (groups, 1), 0, 2) == 1
    own_base = jax.random.randint(key_base, (groups, 1), 0, REGIONS - 1)
    base = jnp.where(shared_flag, common_base, own_base)
    spread = jnp.left_shift(jnp.int32(1), jax.random.randint(key_spread, (groups, 1), 0, 7))
    spread = jnp.where(shared_flag, jnp.int32(1), spread)
    shift_amount = jax.random.randint(key_offset, (groups, ROW_DEV), 0, 1 << 30) % spread
    scattered = 1 + (base + shift_amount) % (REGIONS - 1)
    group_index = jnp.arange(groups, dtype=jnp.int32)[:, None]
    row_place = group_index // N_COL
    col_place = group_index % N_COL
    base_count = ROW_DEV * 9 * (row_place + col_place) // (10 * (N_ROW + N_COL - 2))
    factor = jax.random.randint(key_factor, (groups, 1), 5, 11)
    common_count = (base_count * factor + 9) // 10
    position = jnp.arange(ROW_DEV, dtype=jnp.int32)[None, :]
    labels = jnp.where(position < common_count, 0, scattered).reshape(TOKENS)
    labels = labels.at[TOKENS - 1].set(REGIONS - 1)
    return labels.astype(jnp.int32)


def setup_inputs(seed: int = 0) -> dict:
    keys = jax.random.split(jax.random.key(seed), 7)
    lensed_picture_vectors = draw_lensed_picture_vectors(jax.random.fold_in(keys[6], 71), 0)
    theta_feature_vectors = draw_theta_feature_vectors(jax.random.fold_in(keys[6], 71), 0)
    prior_domain_label = draw_prior_domain_label(jax.random.fold_in(keys[6], 71), 0)
    matched_theta_index = jax.random.permutation(keys[3], TOKENS).astype(jnp.int32)
    affinity_gain = jnp.clip(jax.random.uniform(keys[4], (1,), jnp.float32, 5.0, 15.0), 5.0, 15.0)
    affinity_shift = jnp.clip(jax.random.uniform(keys[5], (1,), jnp.float32, -4.0, -1.0), -4.0, -1.0)
    return dict(lensed_picture_vectors=lensed_picture_vectors, theta_feature_vectors=theta_feature_vectors, prior_domain_label=prior_domain_label, matched_theta_index=matched_theta_index, affinity_gain=affinity_gain, affinity_shift=affinity_shift)


def normalize(embed):
    full = embed.astype(jnp.float32)
    scale = lax.rsqrt(lax.optimization_barrier(jnp.mean(full * full, axis=-1, keepdims=True)) + 1e-06)
    full = full * scale
    return (full, scale, full.astype(jnp.bfloat16))

def backward_norm(dnorm, full, scale):
    return scale * (dnorm - full * lax.optimization_barrier(jnp.mean(dnorm * full, axis=-1, keepdims=True)))

def reference(lensed_picture_vectors, theta_feature_vectors, prior_domain_label, matched_theta_index, affinity_gain, affinity_shift):
    data_full, data_scale, data_norm = normalize(lensed_picture_vectors)
    param_full, param_scale, param_norm = normalize(theta_feature_vectors)
    hidden_size = lensed_picture_vectors.shape[1]
    sharpness_coefficient = affinity_gain[0] / hidden_size
    block = math.gcd(512, TOKENS)
    column_entries = jnp.arange(TOKENS, dtype=jnp.int32)

    def step(carry, index):
        param_acc, loss_acc = carry
        start = (index * block).astype(jnp.int32)
        source_count = lax.dynamic_slice_in_dim(data_norm, start, block, 0)
        source_region = lax.dynamic_slice_in_dim(prior_domain_label, start, block, 0)
        source_subset = lax.dynamic_slice_in_dim(matched_theta_index, start, block, 0)
        similarity_value = jnp.dot(source_count, param_norm.T, preferred_element_type=jnp.float32)
        pair_affinity = sharpness_coefficient * similarity_value + affinity_shift[0]
        positive = source_subset[:, None] == column_entries[None, :]
        retain_mask = positive | (source_region[:, None] != prior_domain_label[None, :])
        polarity_value = jnp.where(positive, 1.0, -1.0).astype(jnp.float32)
        partial_loss = jnp.sum(jnp.where(retain_mask, -jax.nn.log_sigmoid(polarity_value * pair_affinity), 0.0))
        pairwise_slope = (jnp.where(retain_mask, -polarity_value * jax.nn.sigmoid(-polarity_value * pair_affinity), 0.0) * sharpness_coefficient).astype(jnp.bfloat16)
        image_embed_gradient = jnp.dot(pairwise_slope, param_norm, preferred_element_type=jnp.float32)
        param_d = jnp.dot(pairwise_slope.T, source_count, preferred_element_type=jnp.float32)
        return ((param_acc + param_d, loss_acc + partial_loss), image_embed_gradient)
    init = (jnp.zeros((TOKENS, hidden_size), jnp.float32), jnp.zeros((), jnp.float32))
    (param_dnorm, total), data_blocks = lax.scan(step, init, jnp.arange(TOKENS // block, dtype=jnp.int32))
    data_dnorm = data_blocks.reshape(TOKENS, hidden_size)
    loss = (total / (TOKENS * TOKENS)).reshape(1).astype(jnp.float32)
    return (loss, backward_norm(data_dnorm, data_full, data_scale), backward_norm(param_dnorm, param_full, param_scale))
```

```python
import functools

import jax
import jax.numpy as jnp
from jax import lax
from jax.experimental import pallas as pl
from jax.experimental.pallas import tpu as pltpu
from jax.sharding import PartitionSpec as P

AUX = 16
FULL = 32000.0
LOG2E = 1.4426950408889634
LN2 = 0.6931471805599453
VMEM = pl.BlockSpec(memory_space=pltpu.VMEM)
SMEM = pl.BlockSpec(memory_space=pltpu.SMEM)
F32 = jnp.float32
BF16 = jnp.bfloat16
I16 = jnp.int16


def call(body, out_shape, in_specs, scratch=(), aliases=None, vmem=24 * 2**20):
    inner = pl.pallas_call(
        body,
        out_shape=jax.tree.map(lambda s: pltpu.VMEM(s.shape, s.dtype), out_shape),
        in_specs=in_specs,
        input_output_aliases=aliases or {},
        cost_estimate=pl.CostEstimate(flops=1, bytes_accessed=1, transcendentals=0),
        out_specs=jax.tree.map(lambda _: VMEM, out_shape),
        scratch_shapes=list(scratch),
        compiler_params=pltpu.CompilerParams(vmem_limit_bytes=vmem),
    )

    def run(*args):
        args = [
            x if s is SMEM else pltpu.with_memory_space_constraint(x, s.memory_space)
            for x, s in zip(args, in_specs)
        ]
        return inner(*args)

    return run


def normalize(embed):
    full = embed.astype(F32)
    scale = lax.rsqrt(jnp.mean(full * full, axis=-1, keepdims=True) + 1e-06)
    return full * scale, scale


def pack_kernel(data_hbm, param_hbm, region_hbm, partner_hbm, data_msg, param_msg, *scratch):
    data, param, region, partner, aux, sems = scratch
    rows = data.shape[0]
    pairs = ((param_hbm, param), (region_hbm, region), (partner_hbm, partner), (data_hbm, data))
    copies = [pltpu.make_async_copy(a, b, sems.at[i]) for i, (a, b) in enumerate(pairs)]
    for copy in copies:
        copy.start()
    aux[...] = jnp.zeros_like(aux)
    for copy in copies:
        copy.wait()
    index = partner[...]
    aux[0:1, 0:rows] = region[...].astype(F32)
    aux[1:2, 0:rows] = (index >> 8).astype(F32)
    aux[2:3, 0:rows] = (index & 255).astype(F32)
    side = aux[...].astype(BF16)
    for raw, msg in ((param, param_msg), (data, data_msg)):
        msg[pl.ds(rows, AUX), :] = side
        msg[pl.ds(0, rows), :] = normalize(raw[...])[0].astype(BF16)


def encode(value, ref, start):
    rows, width = value.shape
    parts = value.reshape(rows // AUX, AUX, width)
    top = jnp.max(jnp.abs(parts), axis=0)
    power = jnp.ceil(jnp.log2(jnp.maximum(top, 1e-30)) * 256.0)
    unit = jnp.exp2(power * (-1.0 / 256.0)) * FULL
    coded = ((parts * unit[None] + 32768.5).astype(jnp.int32) - 32768).astype(I16)
    ref[pl.ds(start, rows), :] = coded.reshape(rows, width)
    ref[pl.ds(start + rows, AUX), :] = power.astype(jnp.int32).astype(I16)


def decode(ref, start, rows):
    width = ref.shape[-1]
    coded = ref[pl.ds(start, rows), :].astype(F32).reshape(rows // AUX, AUX, width)
    power = ref[pl.ds(start + rows, AUX), :].astype(F32)
    unit = jnp.exp2(power * (1.0 / 256.0)) * (1.0 / FULL)
    return (coded * unit[None]).reshape(rows, width)


def log1p(t):
    u = 1.0 + t
    small = t * (1.0 - t * (0.5 - t * (1.0 / 3.0)))
    return jnp.where(t < 0.01, small, jnp.log(u))


LAST = (((1,), (1,)), ((), ()))
FIRST = (((0,), (0,)), ((), ()))


def load_data(msgs, data, side, rows):
    for i, msg in enumerate(msgs):
        at = pl.ds(i * rows, rows)
        data[at, :] = msg[pl.ds(0, rows), :]
        aux = msg[pl.ds(rows, AUX), :].astype(F32)[:, :rows]
        side[0:1, at] = aux[0:1]
        side[1:2, at] = aux[1:2] * 256.0 + aux[2:3]


def side_columns(msg, base, rows):
    square = (rows + 127) // 128 * 128
    lane = lax.broadcasted_iota(jnp.int32, (rows, square), 1)
    eye = (lax.broadcasted_iota(jnp.int32, (rows, square), 0) == lane).astype(F32).astype(BF16)
    aux = msg[pl.ds(rows, AUX), :][:, :square]
    region = lax.dot_general(eye, aux, LAST, preferred_element_type=F32)[:, 0:1]
    place = lax.broadcasted_iota(jnp.int32, (rows, 1), 0) + base
    return region, place.astype(F32)


def tile(block, columns, data, side, coef, shift):
    region_col, index_col = columns
    rows, cols = block.shape[0], data.shape[0]
    dots = lax.dot_general(block, data[...], LAST, preferred_element_type=F32)
    positive = index_col == side[1:2, :]
    keep = jnp.logical_or(positive, region_col != side[0:1, :])
    x = dots * (coef * LOG2E) + shift * LOG2E
    x = jnp.where(positive, -x, x)
    t = jnp.where(keep, jnp.exp2(x), 0.0)
    slope = t / (1.0 + t)
    grad = (jnp.where(positive, -slope, slope) * coef).astype(BF16)
    q = t.reshape(4, rows // 4, cols)
    t01 = q[0] + q[1] * (1.0 + q[0])
    t23 = q[2] + q[3] * (1.0 + q[2])
    terms = log1p(t01 + t23 * (1.0 + t01)).reshape(rows // 32, 8, cols)
    terms = jnp.sum(terms, axis=0)
    loss = terms[:, 0:128]
    for k in range(128, cols, 128):
        loss = loss + terms[:, k : k + 128]
    return grad, loss


def early_kernel(rows, n, p_n, *refs):
    msgs, params, (base, coef) = refs[:n], refs[n : n + p_n], refs[n + p_n : n + p_n + 2]
    data, side, acc, parts, loss_out = refs[n + p_n + 2 :]
    load_data(msgs, data, side, rows)
    loss = jnp.zeros((8, 128), F32)
    for s in range(p_n):
        block = params[s][pl.ds(0, rows), :]
        columns = side_columns(params[s], base[s], rows)
        grad, term = tile(block, columns, data, side, coef[0], coef[1])
        loss = loss + term
        parts[pl.ds(s * rows, rows), :] = jnp.dot(grad, data[...], preferred_element_type=F32)
        d_part = lax.dot_general(grad, block, FIRST, preferred_element_type=F32)
        acc[...] = d_part if s == 0 else acc[...] + d_part
    loss_out[...] = loss


def middle_kernel(rows, n, p_n, m_n, *refs):
    msgs, params = refs[:n], refs[n : n + p_n + m_n]
    data0, side0, acc0, parts_in, loss_in, base, coef = refs[n + p_n + m_n : n + p_n + m_n + 7]
    data, side, acc0_out, acc, parts, loss_out = refs[n + p_n + m_n + 7 :]
    load_data(msgs, data, side, rows)
    loss = loss_in[...]
    for s in range(p_n + m_n):
        at = pl.ds(s * rows, rows)
        block = params[s][pl.ds(0, rows), :]
        columns = side_columns(params[s], base[s], rows)
        grad, term = tile(block, columns, data, side, coef[0], coef[1])
        loss = loss + term
        part = jnp.dot(grad, data[...], preferred_element_type=F32)
        d_part = lax.dot_general(grad, block, FIRST, preferred_element_type=F32)
        acc[...] = d_part if s == 0 else acc[...] + d_part
        if s < p_n:
            parts[at, :] = parts_in[at, :] + part
            continue
        grad, term = tile(block, columns, data0, side0, coef[0], coef[1])
        loss = loss + term
        parts[at, :] = part + jnp.dot(grad, data0[...], preferred_element_type=F32)
        d_part = lax.dot_general(grad, block, FIRST, preferred_element_type=F32)
        acc0_out[...] = (acc0 if s == p_n else acc0_out)[...] + d_part
    if m_n == 0:
        acc0_out[...] = acc0[...]
    loss_out[...] = loss


def late_kernel(rows, n, l_n, ready, *refs):
    params = refs[:l_n]
    data0, side0, acc0, data1, side1, acc1, parts, loss_in, base, coef = refs[l_n : l_n + 10]
    outs = refs[l_n + 10 :]
    keep_d, send_d, loss_out = outs[:3]
    send_p = outs[3:]
    loss = loss_in[...]
    half = n // 2
    for k, s in enumerate(ready):
        encode(parts[pl.ds(s * rows, rows), :], send_p[k], 0)
    for s in range(l_n):
        block = params[s][pl.ds(0, rows), :]
        columns = side_columns(params[s], base[s], rows)
        total = None
        for h, (data, side, acc) in enumerate(((data0, side0, acc0), (data1, side1, acc1))):
            grad, term = tile(block, columns, data, side, coef[0], coef[1])
            loss = loss + term
            part = jnp.dot(grad, data[...], preferred_element_type=F32)
            total = part if total is None else total + part
            d_part = acc[...] + lax.dot_general(grad, block, FIRST, preferred_element_type=F32)
            if s < l_n - 1:
                acc[...] = d_part
                continue
            for i in range(half):
                keep_d[pl.ds((2 * i + h) * rows, rows), :] = d_part[i * rows : (i + 1) * rows]
                at = half + i
                encode(d_part[at * rows : (at + 1) * rows], send_d, (2 * i + h) * (rows + AUX))
        encode(total, send_p[len(ready) + s], 0)
    loss_out[...] = loss


def emit_kernel(rows, plan, *refs):
    n_arrays = max(max([b] + [a for a, _ in parts]) for b, _, parts in plan) + 1
    arrays, loss, got, outs = refs[:n_arrays], refs[n_arrays], refs[n_arrays + 1], refs[n_arrays + 2 :]
    outs[-1][...] = loss[...] + got[...]
    for out, (b, start, parts) in zip(outs, plan):
        total = arrays[b][pl.ds(start * rows, rows), :]
        for a, i in parts:
            total = total + decode(arrays[a], i * (rows + AUX), rows)
        encode(total, out, 0)


def finish_kernel(rows, plan, pairs, raw_ref, *refs):
    start, parts, arrays = plan
    if pairs:
        terms, out_ref, loss_ref = refs[arrays:-2], refs[-2], refs[-1]
        loss_ref[...] = jnp.sum(sum([t[...] for t in terms]), keepdims=True) / (pairs * pairs)
    else:
        out_ref = refs[-1]
    full, scale = normalize(raw_ref[...])
    dnorm = refs[0][pl.ds(start * rows, rows), :]
    for a, i in parts:
        dnorm = dnorm + decode(refs[a], i * (rows + AUX), rows)
    out_ref[...] = scale * (dnorm - full * jnp.mean(dnorm * full, axis=-1, keepdims=True))


def combine(bits):
    masks = [0]
    for bit in bits:
        masks += [m ^ bit for m in masks]
    return masks


def on_device(core, bits_data, bits_param, sizes, data, param, region, partner, gain, shift):
    rows, width = data.shape
    msg = rows + AUX
    devices = sizes["row"] * sizes["col"]
    shape = jax.ShapeDtypeStruct

    def swap(x, mask):
        return lax.ppermute(x, ("row", "col"), [(i, i ^ mask) for i in range(devices)])

    data_msg, param_msg = call(
        pack_kernel,
        [shape((msg, width), BF16)] * 2,
        [pl.BlockSpec(memory_space=pltpu.HBM)] * 4,
        [
            pltpu.VMEM((rows, width), BF16),
            pltpu.VMEM((rows, width), BF16),
            pltpu.VMEM((1, rows), jnp.int32),
            pltpu.VMEM((1, rows), jnp.int32),
            pltpu.VMEM((AUX, width), F32),
            pltpu.SemaphoreType.DMA((4,)),
        ],
    )(data, param, region.reshape(1, rows), partner.reshape(1, rows))
    held_p, masks_p = [param_msg], [0]
    held_d = [data_msg]
    for k in range(max(len(bits_data), len(bits_param))):
        if k < len(bits_param):
            held_p += [swap(x, bits_param[k]) for x in held_p]
            masks_p += [m ^ bits_param[k] for m in masks_p]
        if k < len(bits_data):
            held_d += [swap(x, bits_data[k]) for x in held_d]
    held_d = [held_d, [swap(x, core) for x in held_d]]
    me = lax.axis_index("row") * sizes["col"] + lax.axis_index("col")
    coef = jnp.stack([gain[0] / width, shift[0]])
    n_own, n_param = len(held_d[0]), len(held_p)
    halves = [[x for side in held_d for x in side[h::2]] for h in (0, 1)]
    n = n_own
    cols = n * rows
    late = [i for i in range(n_param) if i == n_param - 1]
    early = [i for i in range(n_param) if i not in late and not i & 1]
    middle = [i for i in range(n_param) if i not in late and i & 1]
    order = early + middle
    base = {i: (me ^ masks_p[i]) * rows for i in range(n_param)}
    bases = lambda group: jnp.stack([base[i] for i in group]).astype(jnp.int32)
    data0, side0, acc0, parts, loss = call(
        functools.partial(early_kernel, rows, n, len(early)),
        [
            shape((cols, width), BF16),
            shape((8, cols), F32),
            shape((cols, width), F32),
            shape((len(early) * rows, width), F32),
            shape((8, 128), F32),
        ],
        [VMEM] * (n + len(early)) + [SMEM] * 2,
    )(*halves[0], *[held_p[i] for i in early], bases(early), coef)
    data1, side1, acc0, acc1, parts, loss = call(
        functools.partial(middle_kernel, rows, n, len(early), len(middle)),
        [
            shape((cols, width), BF16),
            shape((8, cols), F32),
            shape((cols, width), F32),
            shape((cols, width), F32),
            shape((len(order) * rows, width), F32),
            shape((8, 128), F32),
        ],
        [VMEM] * (n + len(order) + 5) + [SMEM] * 2,
    )(
        *halves[1], *[held_p[i] for i in order], data0, side0, acc0, parts, loss, bases(order), coef
    )
    top = n_param // 2
    ready = [k for k, i in enumerate(order) if i >= top]
    sent = [order[k] for k in ready] + late
    keep_d, send_d, loss, *send_p = call(
        functools.partial(late_kernel, rows, n, len(late), ready),
        [
            shape((n * rows, width), F32),
            shape((n * msg, width), I16),
            shape((8, 128), F32),
            *[shape((msg, width), I16)] * len(sent),
        ],
        [VMEM] * (len(late) + 8) + [SMEM] * 2,
    )(
        *[held_p[i] for i in late],
        data0, side0, acc0, data1, side1, acc1, parts, loss, bases(late), coef,
    )
    loss_steps = [core] + bits_data[:0:-1] + bits_param[:0:-1] + bits_data[:1] + bits_param[:1]
    pending = [swap(loss, loss_steps.pop(0))]

    def emit(items):
        nonlocal loss
        arrays = []

        def slot(x):
            for i, y in enumerate(arrays):
                if x is y:
                    return i
            arrays.append(x)
            return len(arrays) - 1

        plan = [(slot(b), at, [(slot(x), i) for x, i in parts]) for b, at, parts in items]
        *msgs, loss = call(
            functools.partial(emit_kernel, rows, plan),
            [shape((msg, width), I16)] * len(items) + [shape((8, 128), F32)],
            [VMEM] * (len(arrays) + 2),
        )(*arrays, loss, pending.pop())
        if len(loss_steps) > 2 or emits[0] > 1:
            pending.append(swap(loss, loss_steps.pop(0)))
        emits[0] -= 1
        return msgs

    got = swap(send_d, core)
    items_d = [(keep_d, i, [(got, i)]) for i in range(n_own)]
    items_p = [(parts, order.index(i), []) for i in range(top)]
    got = {i: swap(x, bits_param[-1]) for i, x in zip(sent, send_p)}
    for i in range(top):
        items_p[i][2].append((got[i + top], 0))
    left_d, left_p = bits_data[::-1], bits_param[-2::-1]
    emits = [len(left_d) + len(left_p)]
    while left_d or left_p:
        for items, left in ((items_d, left_d), (items_p, left_p)):
            if left:
                step, half = left.pop(0), len(items) // 2
                for i, x in enumerate(emit(items[half:])):
                    items[i][2].append((swap(x, step), 0))
                del items[half:]
    while len(loss_steps) > 2:
        loss = loss + pending.pop()
        pending.append(swap(loss, loss_steps.pop(0)))
    if pending:
        loss = loss + pending.pop()
    terms = [loss] + [swap(loss, m) for m in combine(loss_steps)[1:]]

    def finish(raw, item, terms=(), pairs=0):
        arrays, at, parts = [item[0]], item[1], []
        for x, i in item[2]:
            arrays.append(x)
            parts.append((len(arrays) - 1, i))
        return call(
            functools.partial(finish_kernel, rows, (at, parts, len(arrays)), pairs),
            [shape((rows, width), F32)] + [shape((1, 1), F32)] * bool(pairs),
            [VMEM] * (1 + len(arrays) + len(terms)),
        )(raw, *arrays, *terms)

    (grad_param,) = finish(param, items_p[0])
    grad_data, loss = finish(data, items_d[0], terms, rows * devices)
    return loss.reshape(1), grad_data, grad_param


def solution(mesh):
    sizes = dict(mesh.shape)
    columns = sizes["col"]
    col_bits = [1 << k for k in range(columns.bit_length() - 1)]
    row_bits = [columns << k for k in range(sizes["row"].bit_length() - 1)]
    core, rest = col_bits[0], col_bits[1:]
    bits_data = row_bits[0::2] + rest[0::2]
    bits_param = row_bits[1::2] + rest[1::2]
    split = P(("row", "col"))
    rows = P(("row", "col"), None)
    return jax.shard_map(
        functools.partial(on_device, core, bits_data, bits_param, sizes),
        mesh=mesh,
        in_specs=(rows, rows, split, split, P(), P()),
        out_specs=(P(), rows, rows),
        check_vma=False,
    )
```

```python
import functools

import jax
import jax.numpy as jnp
from jax import lax
from jax.experimental import pallas as pl
from jax.experimental.pallas import tpu as pltpu
from jax.sharding import PartitionSpec as P

AUX = 16
SUB = 8
FULL = 32000.0
LIMB = 16384.0
LOG2E = 1.4426950408889634
LN2 = 0.6931471805599453
VMEM = pl.BlockSpec(memory_space=pltpu.VMEM)
SMEM = pl.BlockSpec(memory_space=pltpu.SMEM)
F32 = jnp.float32
BF16 = jnp.bfloat16
I16 = jnp.int16


def call(body, out_shape, in_specs, scratch=(), aliases=None, vmem=16 * 2**20, to=pltpu.VMEM):
    inner = pl.pallas_call(
        body,
        out_shape=jax.tree.map(lambda s: to(s.shape, s.dtype), out_shape),
        in_specs=in_specs,
        input_output_aliases=aliases or {},
        cost_estimate=pl.CostEstimate(flops=1, bytes_accessed=1, transcendentals=0),
        out_specs=jax.tree.map(lambda _: pl.BlockSpec(memory_space=to), out_shape),
        scratch_shapes=list(scratch),
        compiler_params=pltpu.CompilerParams(vmem_limit_bytes=vmem),
    )

    def run(*args):
        args = [
            x if s is SMEM else pltpu.with_memory_space_constraint(x, s.memory_space)
            for x, s in zip(args, in_specs)
        ]
        return inner(*args)

    return run


def normalize(embed):
    full = embed.astype(F32)
    scale = lax.rsqrt(jnp.mean(full * full, axis=-1, keepdims=True) + 1e-06)
    return full * scale, scale


def pack_kernel(data_hbm, param_hbm, region_hbm, partner_hbm, param_msg, data, side, *scratch):
    param, region, partner, aux, sems = scratch
    rows = data.shape[0]
    pairs = ((param_hbm, param), (region_hbm, region), (partner_hbm, partner), (data_hbm, data))
    copies = [pltpu.make_async_copy(a, b, sems.at[i]) for i, (a, b) in enumerate(pairs)]
    for copy in copies:
        copy.start()
    aux[...] = jnp.zeros_like(aux)
    for copy in copies:
        copy.wait()
    index = partner[...]
    aux[0:1, 0:rows] = region[...].astype(F32)
    aux[1:2, 0:rows] = (index >> 8).astype(F32)
    aux[2:3, 0:rows] = (index & 255).astype(F32)
    side[...] = aux[...].astype(BF16)
    param_msg[pl.ds(rows, AUX), :] = side[...]
    param_msg[pl.ds(0, rows), :] = normalize(param[...])[0].astype(BF16)


def pack_data_kernel(data, side, data_msg):
    rows = data.shape[0]
    data_msg[pl.ds(rows, AUX), :] = side[...]
    data_msg[pl.ds(0, rows), :] = normalize(data[...])[0].astype(BF16)


def encode(value, ref, start, loss=None):
    rows, width = value.shape
    parts = value.reshape(rows // SUB, SUB, width)
    top = jnp.max(jnp.abs(parts), axis=0)
    power = jnp.ceil(jnp.log2(jnp.maximum(top, 1e-30)) * 256.0)
    unit = jnp.exp2(power * (-1.0 / 256.0)) * FULL
    coded = ((parts * unit[None] + 32768.5).astype(jnp.int32) - 32768).astype(I16)
    ref[pl.ds(start, rows), :] = coded.reshape(rows, width)
    below = jnp.zeros_like(power)
    if loss is not None:
        exponent = jnp.ceil(jnp.log2(jnp.maximum(loss, 1e-30)))
        mantissa = loss * jnp.exp2(-exponent) * LIMB
        high = jnp.floor(mantissa)
        low = jnp.floor((mantissa - high) * LIMB)
        rest = jnp.zeros((SUB, width - 3 * loss.shape[1]), F32)
        below = jnp.concatenate([exponent, high, low, rest], axis=1)
    aux = jnp.concatenate([power, below], axis=0)
    ref[pl.ds(start + rows, AUX), :] = aux.astype(jnp.int32).astype(I16)


def decode(ref, start, rows, at=0, piece=None):
    piece, width = piece or rows, ref.shape[-1]
    coded = ref[pl.ds(start + at, piece), :].astype(F32).reshape(piece // SUB, SUB, width)
    power = ref[pl.ds(start + rows, AUX), :].astype(F32)[:SUB]
    unit = jnp.exp2(power * (1.0 / 256.0)) * (1.0 / FULL)
    return (coded * unit[None]).reshape(piece, width)


def decode_loss(ref, rows):
    exponent, high, low = jnp.split(ref[pl.ds(rows, AUX), :].astype(F32)[SUB:, :384], 3, axis=1)
    return (high + low * (1.0 / LIMB)) * (1.0 / LIMB) * jnp.exp2(exponent)


def log1p(t):
    u = 1.0 + t
    small = t * (1.0 - t * (0.5 - t * (1.0 / 3.0)))
    return jnp.where(t < 0.01, small, jnp.log(u))


LAST = (((1,), (1,)), ((), ()))
FIRST = (((0,), (0,)), ((), ()))


def load_data(msgs, data, side, rows):
    for i, msg in enumerate(msgs):
        at = pl.ds(i * rows, rows)
        data[at, :] = msg[pl.ds(0, rows), :]
        aux = msg[pl.ds(rows, AUX), :].astype(F32)[:, :rows]
        side[0:1, at] = aux[0:1]
        side[1:2, at] = aux[1:2] * 256.0 + aux[2:3]


def side_columns(msg, base, rows):
    square = (rows + 127) // 128 * 128
    lane = lax.broadcasted_iota(jnp.int32, (rows, square), 1)
    eye = (lax.broadcasted_iota(jnp.int32, (rows, square), 0) == lane).astype(F32).astype(BF16)
    aux = msg[pl.ds(rows, AUX), :][:, :square]
    region = lax.dot_general(eye, aux, LAST, preferred_element_type=F32)[:, 0:1]
    place = lax.broadcasted_iota(jnp.int32, (rows, 1), 0) + base
    return region, place.astype(F32)


def tile(block, columns, data, side, coef, shift):
    region_col, index_col = columns
    rows, cols = block.shape[0], data.shape[0]
    dots = lax.dot_general(block, data[...], LAST, preferred_element_type=F32)
    positive = index_col == side[1:2, :]
    keep = jnp.logical_or(positive, region_col != side[0:1, :])
    x = dots * (coef * LOG2E) + shift * LOG2E
    x = jnp.where(positive, -x, x)
    t = jnp.where(keep, jnp.exp2(x), 0.0)
    slope = t / (1.0 + t)
    grad = (jnp.where(positive, -slope, slope) * coef).astype(BF16)
    q = t.reshape(4, rows // 4, cols)
    t01 = q[0] + q[1] * (1.0 + q[0])
    t23 = q[2] + q[3] * (1.0 + q[2])
    terms = log1p(t01 + t23 * (1.0 + t01)).reshape(rows // 32, 8, cols)
    terms = jnp.sum(terms, axis=0)
    loss = terms[:, 0:128]
    for k in range(128, cols, 128):
        loss = loss + terms[:, k : k + 128]
    return grad, loss


def early_kernel(rows, n, p_n, *refs):
    msgs, params, (base, coef) = refs[:n], refs[n : n + p_n], refs[n + p_n : n + p_n + 2]
    data, side, acc, loss_out = refs[n + p_n + 2 :]
    cols = n * rows
    load_data(msgs, data, side, rows)
    loss = jnp.zeros((8, 128), F32)
    for s in range(p_n):
        block = params[s][pl.ds(0, rows), :]
        columns = side_columns(params[s], base[s], rows)
        grad, term = tile(block, columns, data, side, coef[0], coef[1])
        loss = loss + term
        at = pl.ds(cols + s * rows, rows)
        acc[at, :] = jnp.dot(grad, data[...], preferred_element_type=F32)
        d_part = lax.dot_general(grad, block, FIRST, preferred_element_type=F32)
        acc[pl.ds(0, cols), :] = d_part if s == 0 else acc[pl.ds(0, cols), :] + d_part
    loss_out[...] = loss


def middle_kernel(rows, n, p_n, m_n, *refs):
    msgs, params = refs[:n], refs[n : n + p_n + m_n]
    data0, side0, acc0, loss_in, base, coef = refs[n + p_n + m_n : n + p_n + m_n + 6]
    data, side, acc0_out, acc, parts, loss_out = refs[n + p_n + m_n + 6 :]
    cols = n * rows
    whole = pl.ds(0, cols)
    load_data(msgs, data, side, rows)
    loss = loss_in[...]
    for s in range(p_n + m_n):
        at = pl.ds(s * rows, rows)
        block = params[s][pl.ds(0, rows), :]
        columns = side_columns(params[s], base[s], rows)
        grad, term = tile(block, columns, data, side, coef[0], coef[1])
        loss = loss + term
        part = jnp.dot(grad, data[...], preferred_element_type=F32)
        d_part = lax.dot_general(grad, block, FIRST, preferred_element_type=F32)
        acc[...] = d_part if s == 0 else acc[...] + d_part
        if s < p_n:
            parts[at, :] = acc0[pl.ds(cols + s * rows, rows), :] + part
            continue
        grad, term = tile(block, columns, data0, side0, coef[0], coef[1])
        loss = loss + term
        parts[at, :] = part + jnp.dot(grad, data0[...], preferred_element_type=F32)
        d_part = lax.dot_general(grad, block, FIRST, preferred_element_type=F32)
        acc0_out[...] = (acc0[whole, :] if s == p_n else acc0_out[...]) + d_part
    if m_n == 0:
        acc0_out[...] = acc0[whole, :]
    loss_out[...] = loss


def late_kernel(rows, n, l_n, ready, *refs):
    params = refs[:l_n]
    data0, side0, acc0, data1, side1, acc1, parts, loss_in, base, coef = refs[l_n : l_n + 10]
    outs = refs[l_n + 10 :]
    keep_d, send_d, loss_out = outs[:3]
    send_p = outs[3:]
    loss = loss_in[...]
    half = n // 2
    for k, s in enumerate(ready):
        encode(parts[pl.ds(s * rows, rows), :], send_p[k], 0)
    for s in range(l_n):
        block = params[s][pl.ds(0, rows), :]
        columns = side_columns(params[s], base[s], rows)
        total = None
        for h, (data, side, acc) in enumerate(((data0, side0, acc0), (data1, side1, acc1))):
            grad, term = tile(block, columns, data, side, coef[0], coef[1])
            loss = loss + term
            part = jnp.dot(grad, data[...], preferred_element_type=F32)
            total = part if total is None else total + part
            d_part = acc[...] + lax.dot_general(grad, block, FIRST, preferred_element_type=F32)
            if s < l_n - 1:
                acc[...] = d_part
                continue
            for i in range(half):
                keep_d[pl.ds((2 * i + h) * rows, rows), :] = d_part[i * rows : (i + 1) * rows]
                at = half + i
                encode(d_part[at * rows : (at + 1) * rows], send_d, (2 * i + h) * (rows + AUX))
        encode(total, send_p[len(ready) + s], 0)
    loss_out[...] = loss


def emit_kernel(rows, plan, n_arrays, carried, *refs):
    arrays, terms, outs = refs[:n_arrays], refs[n_arrays:], None
    loss = None
    if carried is None:
        outs = terms
    else:
        terms, outs = terms[: -len(plan) - 1], terms[-len(plan) - 1 :]
        loss = sum([t[...] for t in terms] + [decode_loss(arrays[a], rows) for a in carried])
        outs[-1][...] = loss
    for out, (b, start, parts) in zip(outs, plan):
        total = arrays[b][pl.ds(start * rows, rows), :]
        for a, i in parts:
            total = total + decode(arrays[a], i * (rows + AUX), rows)
        encode(total, out, 0, loss)


def finish_kernel(rows, plan, pairs, raw_ref, *refs):
    start, parts, arrays, carried = plan
    out_vmem, loss_vmem, sems = refs[-3:]
    out_ref = refs[-5] if pairs else refs[-4]
    copies = []
    if pairs:
        terms = [t[...] for t in refs[arrays:-5]] + [decode_loss(refs[a], rows) for a in carried]
        loss_vmem[...] = jnp.sum(sum(terms), keepdims=True) / (pairs * pairs)
        copies.append(pltpu.make_async_copy(loss_vmem, refs[-4], sems.at[0]))
        copies[-1].start()
    piece = rows // 3 if rows % (3 * AUX) == 0 else rows
    for k, at in enumerate(range(0, rows, piece)):
        full, scale = normalize(raw_ref[pl.ds(at, piece), :])
        dnorm = refs[0][pl.ds(start * rows + at, piece), :]
        for a, i in parts:
            dnorm = dnorm + decode(refs[a], i * (rows + AUX), rows, at, piece)
        grad = scale * (dnorm - full * jnp.mean(dnorm * full, axis=-1, keepdims=True))
        here = pl.ds(at, piece)
        out_vmem[here, :] = grad
        copies.append(pltpu.make_async_copy(out_vmem.at[here], out_ref.at[here], sems.at[1 + k]))
        copies[-1].start()
    for copy in copies:
        copy.wait()


def combine(bits):
    masks = [0]
    for bit in bits:
        masks += [m ^ bit for m in masks]
    return masks


def on_device(core, bits_data, bits_param, sizes, data, param, region, partner, gain, shift):
    rows, width = data.shape
    msg = rows + AUX
    devices = sizes["row"] * sizes["col"]
    shape = jax.ShapeDtypeStruct

    def swap(x, mask):
        return lax.ppermute(x, ("row", "col"), [(i, i ^ mask) for i in range(devices)])

    param_msg, raw_data, side = call(
        pack_kernel,
        [shape((msg, width), BF16), shape((rows, width), BF16), shape((AUX, width), BF16)],
        [pl.BlockSpec(memory_space=pltpu.HBM)] * 4,
        [
            pltpu.VMEM((rows, width), BF16),
            pltpu.VMEM((1, rows), jnp.int32),
            pltpu.VMEM((1, rows), jnp.int32),
            pltpu.VMEM((AUX, width), F32),
            pltpu.SemaphoreType.DMA((4,)),
        ],
    )(data, param, region.reshape(1, rows), partner.reshape(1, rows))
    (data_msg,) = call(pack_data_kernel, [shape((msg, width), BF16)], [VMEM] * 2)(raw_data, side)
    held_p, masks_p = [param_msg], [0]
    held_d = [data_msg]
    for k in range(max(len(bits_data), len(bits_param))):
        if k < len(bits_param):
            held_p += [swap(x, bits_param[k]) for x in held_p]
            masks_p += [m ^ bits_param[k] for m in masks_p]
        if k < len(bits_data):
            held_d += [swap(x, bits_data[k]) for x in held_d]
    n_own, n_param = len(held_d), len(held_p)
    other_d = [swap(x, core) for x in held_d]
    me = lax.axis_index("row") * sizes["col"] + lax.axis_index("col")
    coef = jnp.stack([gain[0] / width, shift[0]])
    n = n_own
    cols = n * rows
    late = [i for i in range(n_param) if i == n_param - 1]
    early = [i for i in range(n_param) if i not in late and not i & 1]
    middle = [i for i in range(n_param) if i not in late and i & 1]
    order = early + middle
    base = {i: (me ^ masks_p[i]) * rows for i in range(n_param)}
    bases = lambda group: jnp.stack([base[i] for i in group]).astype(jnp.int32)
    data0, side0, acc0, loss = call(
        functools.partial(early_kernel, rows, n, len(early)),
        [
            shape((cols, width), BF16),
            shape((8, cols), F32),
            shape((cols + len(early) * rows, width), F32),
            shape((8, 128), F32),
        ],
        [VMEM] * (n + len(early)) + [SMEM] * 2,
    )(*held_d[0::2], *other_d[0::2], *[held_p[i] for i in early], bases(early), coef)
    data1, side1, acc0, acc1, parts, loss = call(
        functools.partial(middle_kernel, rows, n, len(early), len(middle)),
        [
            shape((cols, width), BF16),
            shape((8, cols), F32),
            shape((cols, width), F32),
            shape((cols, width), F32),
            shape((len(order) * rows, width), F32),
            shape((8, 128), F32),
        ],
        [VMEM] * (n + len(order) + 4) + [SMEM] * 2,
    )(
        *held_d[1::2], *other_d[1::2], *[held_p[i] for i in order], data0, side0, acc0, loss, bases(order), coef
    )
    top = n_param // 2
    ready = [k for k, i in enumerate(order) if i >= top]
    sent = [order[k] for k in ready] + late
    keep_d, send_d, loss, *send_p = call(
        functools.partial(late_kernel, rows, n, len(late), ready),
        [
            shape((n * rows, width), F32),
            shape((n * msg, width), I16),
            shape((8, 128), F32),
            *[shape((msg, width), I16)] * len(sent),
        ],
        [VMEM] * (len(late) + 8) + [SMEM] * 2,
    )(
        *[held_p[i] for i in late],
        data0, side0, acc0, data1, side1, acc1, parts, loss, bases(late), coef,
    )
    columns = sizes["col"]
    inner = [b for b in bits_data + bits_param if b < columns]
    outer = [b for b in bits_data + bits_param if b >= columns]
    rounds = [inner, outer]
    terms, carriers = [loss, swap(loss, core)], []

    def emit(items, step, with_loss):
        nonlocal terms, carriers
        arrays = []

        def slot(x):
            for i, y in enumerate(arrays):
                if x is y:
                    return i
            arrays.append(x)
            return len(arrays) - 1

        plan = [(slot(b), at, [(slot(x), i) for x, i in parts]) for b, at, parts in items]
        carried, outs = None, [shape((msg, width), I16)] * len(items)
        n_arrays = len(arrays)
        if with_loss and rounds:
            carried = [slot(x) for x in carriers]
            n_arrays = len(arrays)
            outs.append(shape((8, 128), F32))
            arrays = arrays + terms
        msgs = call(
            functools.partial(emit_kernel, rows, plan, n_arrays, carried),
            outs,
            [VMEM] * len(arrays),
        )(*arrays)
        got = [swap(x, step) for x in msgs[: len(items)]]
        if carried is not None:
            bits = rounds.pop(0)
            terms = [msgs[-1]] + [swap(msgs[-1], m) for m in combine(bits)[1:] if m != step]
            carriers = got[-1:] if step in bits else []
        return got

    got = swap(send_d, core)
    items_d = [(keep_d, i, [(got, i)]) for i in range(n_own)]
    items_p = [(parts, order.index(i), []) for i in range(top)]
    got = {i: swap(x, bits_param[-1]) for i, x in zip(sent, send_p)}
    for i in range(top):
        items_p[i][2].append((got[i + top], 0))
    left_d, left_p = bits_data[::-1], bits_param[-2::-1]
    while left_d or left_p:
        for items, left in ((items_d, left_d), (items_p, left_p)):
            if left:
                step, half = left.pop(0), len(items) // 2
                for i, x in enumerate(emit(items[half:], step, items is items_d)):
                    items[i][2].append((x, 0))
                del items[half:]
    def finish(raw, item, terms=(), carriers=(), pairs=0):
        arrays, at, parts = [item[0]], item[1], []
        for x, i in item[2]:
            arrays.append(x)
            parts.append((len(arrays) - 1, i))
        carried = []
        for x in carriers:
            places = [a for a, y in enumerate(arrays) if y is x]
            if not places:
                arrays.append(x)
            carried.append(places[0] if places else len(arrays) - 1)
        return call(
            functools.partial(finish_kernel, rows, (at, parts, len(arrays), carried), pairs),
            [shape((rows, width), F32)] + [shape((1, 1), F32)] * bool(pairs),
            [VMEM] * (1 + len(arrays) + len(terms)),
            [
                pltpu.VMEM((rows, width), F32),
                pltpu.VMEM((1, 1), F32),
                pltpu.SemaphoreType.DMA((4,)),
            ],
            to=pltpu.HBM,
        )(raw, *arrays, *terms)

    (grad_param,) = finish(param, items_p[0])
    grad_data, loss = finish(data, items_d[0], terms, carriers, rows * devices)
    return loss.reshape(1), grad_data, grad_param


def solution(mesh):
    sizes = dict(mesh.shape)
    columns = sizes["col"]
    col_bits = [1 << k for k in range(columns.bit_length() - 1)]
    row_bits = [columns << k for k in range(sizes["row"].bit_length() - 1)]
    core, rest = col_bits[0], col_bits[1:]
    odd = len(row_bits) & 1
    bits_data = row_bits[0::2] + rest[odd::2]
    bits_param = row_bits[1::2] + rest[1 - odd :: 2]
    split = P(("row", "col"))
    rows = P(("row", "col"), None)
    return jax.shard_map(
        functools.partial(on_device, core, bits_data, bits_param, sizes),
        mesh=mesh,
        in_specs=(rows, rows, split, split, P(), P()),
        out_specs=(P(), rows, rows),
        check_vma=False,
    )
```

```python
import functools

import jax
import jax.numpy as jnp
from jax import lax
from jax.experimental import pallas as pl
from jax.experimental.pallas import tpu as pltpu
from jax.sharding import PartitionSpec as P

AUX = 16
SUB = 8
FULL = 32000.0
LIMB = 16384.0
LOG2E = 1.4426950408889634
LN2 = 0.6931471805599453
VMEM = pl.BlockSpec(memory_space=pltpu.VMEM)
SMEM = pl.BlockSpec(memory_space=pltpu.SMEM)
F32 = jnp.float32
BF16 = jnp.bfloat16
I16 = jnp.int16


def call(body, out_shape, in_specs, scratch=(), aliases=None, vmem=16 * 2**20, to=pltpu.VMEM):
    inner = pl.pallas_call(
        body,
        out_shape=jax.tree.map(lambda s: to(s.shape, s.dtype), out_shape),
        in_specs=in_specs,
        input_output_aliases=aliases or {},
        cost_estimate=pl.CostEstimate(flops=1, bytes_accessed=1, transcendentals=0),
        out_specs=jax.tree.map(lambda _: pl.BlockSpec(memory_space=to), out_shape),
        scratch_shapes=list(scratch),
        compiler_params=pltpu.CompilerParams(vmem_limit_bytes=vmem),
    )

    def run(*args):
        args = [
            x if s is SMEM else pltpu.with_memory_space_constraint(x, s.memory_space)
            for x, s in zip(args, in_specs)
        ]
        return inner(*args)

    return run


def normalize(embed):
    full = embed.astype(F32)
    scale = lax.rsqrt(jnp.mean(full * full, axis=-1, keepdims=True) + 1e-06)
    return full * scale, scale


def pack_kernel(data_hbm, param_hbm, region_hbm, partner_hbm, param_msg, data, side, *scratch):
    param, region, partner, aux, sems = scratch
    rows = data.shape[0]
    pairs = ((param_hbm, param), (region_hbm, region), (partner_hbm, partner), (data_hbm, data))
    copies = [pltpu.make_async_copy(a, b, sems.at[i]) for i, (a, b) in enumerate(pairs)]
    for copy in copies:
        copy.start()
    aux[...] = jnp.zeros_like(aux)
    for copy in copies:
        copy.wait()
    index = partner[...]
    aux[0:1, 0:rows] = region[...].astype(F32)
    aux[1:2, 0:rows] = (index >> 8).astype(F32)
    aux[2:3, 0:rows] = (index & 255).astype(F32)
    side[...] = aux[...].astype(BF16)
    param_msg[pl.ds(rows, AUX), :] = side[...]
    param_msg[pl.ds(0, rows), :] = normalize(param[...])[0].astype(BF16)


def pack_data_kernel(data, side, data_msg):
    rows = data.shape[0]
    data_msg[pl.ds(rows, AUX), :] = side[...]
    data_msg[pl.ds(0, rows), :] = normalize(data[...])[0].astype(BF16)


def encode(value, ref, start, loss=None):
    rows, width = value.shape
    parts = value.reshape(rows // SUB, SUB, width)
    top = jnp.max(jnp.abs(parts), axis=0)
    power = jnp.ceil(jnp.log2(jnp.maximum(top, 1e-30)) * 256.0)
    unit = jnp.exp2(power * (-1.0 / 256.0)) * FULL
    coded = ((parts * unit[None] + 32768.5).astype(jnp.int32) - 32768).astype(I16)
    ref[pl.ds(start, rows), :] = coded.reshape(rows, width)
    below = jnp.zeros_like(power)
    if loss is not None:
        exponent = jnp.ceil(jnp.log2(jnp.maximum(loss, 1e-30)))
        mantissa = loss * jnp.exp2(-exponent) * LIMB
        high = jnp.floor(mantissa)
        low = jnp.floor((mantissa - high) * LIMB)
        rest = jnp.zeros((SUB, width - 3 * loss.shape[1]), F32)
        below = jnp.concatenate([exponent, high, low, rest], axis=1)
    aux = jnp.concatenate([power, below], axis=0)
    ref[pl.ds(start + rows, AUX), :] = aux.astype(jnp.int32).astype(I16)


def decode(ref, start, rows, at=0, piece=None):
    piece, width = piece or rows, ref.shape[-1]
    coded = ref[pl.ds(start + at, piece), :].astype(F32).reshape(piece // SUB, SUB, width)
    power = ref[pl.ds(start + rows, AUX), :].astype(F32)[:SUB]
    unit = jnp.exp2(power * (1.0 / 256.0)) * (1.0 / FULL)
    return (coded * unit[None]).reshape(piece, width)


def decode_loss(ref):
    aux = pl.ds(ref.shape[0] - AUX, AUX)
    exponent, high, low = jnp.split(ref[aux, :].astype(F32)[SUB:, :384], 3, axis=1)
    return (high + low * (1.0 / LIMB)) * (1.0 / LIMB) * jnp.exp2(exponent)


def log1p(t):
    u = 1.0 + t
    small = t * (1.0 - t * (0.5 - t * (1.0 / 3.0)))
    return jnp.where(t < 0.01, small, jnp.log(u))


LAST = (((1,), (1,)), ((), ()))
FIRST = (((0,), (0,)), ((), ()))


def load_data(msgs, data, side, rows):
    for i, msg in enumerate(msgs):
        at = pl.ds(i * rows, rows)
        data[at, :] = msg[pl.ds(0, rows), :]
        aux = msg[pl.ds(rows, AUX), :].astype(F32)[:, :rows]
        side[0:1, at] = aux[0:1]
        side[1:2, at] = aux[1:2] * 256.0 + aux[2:3]


def side_columns(msg, base, rows):
    square = (rows + 127) // 128 * 128
    lane = lax.broadcasted_iota(jnp.int32, (rows, square), 1)
    eye = (lax.broadcasted_iota(jnp.int32, (rows, square), 0) == lane).astype(F32).astype(BF16)
    aux = msg[pl.ds(rows, AUX), :][:, :square]
    region = lax.dot_general(eye, aux, LAST, preferred_element_type=F32)[:, 0:1]
    place = lax.broadcasted_iota(jnp.int32, (rows, 1), 0) + base
    return region, place.astype(F32)


def tile(block, columns, data, side, coef, shift):
    region_col, index_col = columns
    rows, cols = block.shape[0], data.shape[0]
    dots = lax.dot_general(block, data[...], LAST, preferred_element_type=F32)
    positive = index_col == side[1:2, :]
    keep = jnp.logical_or(positive, region_col != side[0:1, :])
    x = dots * (coef * LOG2E) + shift * LOG2E
    x = jnp.where(positive, -x, x)
    t = jnp.where(keep, jnp.exp2(x), 0.0)
    slope = t / (1.0 + t)
    grad = (jnp.where(positive, -slope, slope) * coef).astype(BF16)
    q = t.reshape(4, rows // 4, cols)
    t01 = q[0] + q[1] * (1.0 + q[0])
    t23 = q[2] + q[3] * (1.0 + q[2])
    terms = log1p(t01 + t23 * (1.0 + t01)).reshape(rows // 32, 8, cols)
    terms = jnp.sum(terms, axis=0)
    loss = terms[:, 0:128]
    for k in range(128, cols, 128):
        loss = loss + terms[:, k : k + 128]
    return grad, loss


def scalars(refs, masks, columns_n, rows, width):
    me = lax.axis_index("row") * columns_n + lax.axis_index("col")
    return [(me ^ m) * rows for m in masks], (refs[0][0] * (1.0 / width), refs[1][0])


def tables(refs, masks, columns_n, rows, width):
    return [refs[0][i] for i in range(len(masks))], (refs[1][0], refs[1][1])


def early_kernel(rows, n, masks, columns_n, *refs):
    p_n = len(masks)
    msgs, params = refs[:n], refs[n : n + p_n]
    width = msgs[0].shape[1]
    base, coef = tables(refs[n + p_n : n + p_n + 2], masks, columns_n, rows, width)
    data, side, acc, loss_out = refs[n + p_n + 2 :]
    cols = n * rows
    load_data(msgs, data, side, rows)
    loss = jnp.zeros((8, 128), F32)
    for s in range(p_n):
        block = params[s][pl.ds(0, rows), :]
        columns = side_columns(params[s], base[s], rows)
        grad, term = tile(block, columns, data, side, coef[0], coef[1])
        loss = loss + term
        at = pl.ds(cols + s * rows, rows)
        acc[at, :] = jnp.dot(grad, data[...], preferred_element_type=F32)
        d_part = lax.dot_general(grad, block, FIRST, preferred_element_type=F32)
        acc[pl.ds(0, cols), :] = d_part if s == 0 else acc[pl.ds(0, cols), :] + d_part
    loss_out[...] = loss


def middle_kernel(rows, n, p_n, masks, columns_n, *refs):
    m_n = len(masks) - p_n
    msgs, params = refs[:n], refs[n : n + p_n + m_n]
    data0, side0, acc0, loss_in = refs[n + p_n + m_n : n + p_n + m_n + 4]
    width = msgs[0].shape[1]
    base, coef = scalars(refs[n + p_n + m_n + 4 : n + p_n + m_n + 6], masks, columns_n, rows, width)
    data, side, acc0_out, acc, parts, loss_out = refs[n + p_n + m_n + 6 :]
    cols = n * rows
    whole = pl.ds(0, cols)
    load_data(msgs, data, side, rows)
    loss = loss_in[...]
    for s in range(p_n + m_n):
        at = pl.ds(s * rows, rows)
        block = params[s][pl.ds(0, rows), :]
        columns = side_columns(params[s], base[s], rows)
        grad, term = tile(block, columns, data, side, coef[0], coef[1])
        loss = loss + term
        part = jnp.dot(grad, data[...], preferred_element_type=F32)
        d_part = lax.dot_general(grad, block, FIRST, preferred_element_type=F32)
        acc[...] = d_part if s == 0 else acc[...] + d_part
        if s < p_n:
            parts[at, :] = acc0[pl.ds(cols + s * rows, rows), :] + part
            continue
        grad, term = tile(block, columns, data0, side0, coef[0], coef[1])
        loss = loss + term
        parts[at, :] = part + jnp.dot(grad, data0[...], preferred_element_type=F32)
        d_part = lax.dot_general(grad, block, FIRST, preferred_element_type=F32)
        acc0_out[...] = (acc0[whole, :] if s == p_n else acc0_out[...]) + d_part
    if m_n == 0:
        acc0_out[...] = acc0[whole, :]
    loss_out[...] = loss


def late_kernel(rows, n, masks, columns_n, ready, *refs):
    l_n = len(masks)
    params = refs[:l_n]
    data0, side0, acc0, data1, side1, acc1, parts, loss_in = refs[l_n : l_n + 8]
    width = params[0].shape[1]
    base, coef = scalars(refs[l_n + 8 : l_n + 10], masks, columns_n, rows, width)
    outs = refs[l_n + 10 :]
    keep_d, low_d, top_d, loss_out = outs[:4]
    send_p = outs[4:]
    loss = loss_in[...]
    half = n // 2
    for k, s in enumerate(ready):
        encode(parts[pl.ds(s * rows, rows), :], send_p[k], 0)
    for s in range(l_n):
        block = params[s][pl.ds(0, rows), :]
        columns = side_columns(params[s], base[s], rows)
        total = None
        for h, (data, side, acc) in enumerate(((data0, side0, acc0), (data1, side1, acc1))):
            grad, term = tile(block, columns, data, side, coef[0], coef[1])
            loss = loss + term
            part = jnp.dot(grad, data[...], preferred_element_type=F32)
            total = part if total is None else total + part
            d_part = acc[...] + lax.dot_general(grad, block, FIRST, preferred_element_type=F32)
            if s < l_n - 1:
                acc[...] = d_part
                continue
            for i in range(half):
                place = 2 * i + h
                keep_d[pl.ds(place * rows, rows), :] = d_part[i * rows : (i + 1) * rows]
                send_d = top_d if place >= half else low_d
                at = half + i
                part = d_part[at * rows : (at + 1) * rows]
                with_loss = loss if place == n - 1 else None
                encode(part, send_d, place % half * (rows + AUX), with_loss)
        encode(total, send_p[len(ready) + s], 0)
    loss_out[...] = loss


def emit_kernel(rows, plan, n_arrays, carried, *refs):
    arrays, terms, outs = refs[:n_arrays], refs[n_arrays:], None
    loss = None
    if carried is None:
        outs = terms
    else:
        terms, outs = terms[: -len(plan) - 1], terms[-len(plan) - 1 :]
        loss = sum([t[...] for t in terms] + [decode_loss(arrays[a]) for a in carried])
        outs[-1][...] = loss
    for out, (b, start, parts) in zip(outs, plan):
        total = arrays[b][pl.ds(start * rows, rows), :]
        for a, i in parts:
            total = total + decode(arrays[a], i * (rows + AUX), rows)
        encode(total, out, 0, loss)


def finish_kernel(rows, plans, n_arrays, carried, pairs, *refs):
    arrays, terms, outs = refs[:n_arrays], refs[n_arrays:-7], refs[-7:-4]
    buffers, loss_vmem, sems = refs[-4:-2], refs[-2], refs[-1]
    copies = []

    def send(a, b):
        copies.append(pltpu.make_async_copy(a, b, sems.at[len(copies)]))
        copies[-1].start()

    piece = rows // 3 if rows % (3 * AUX) == 0 else rows
    for k, (raw, base, start, parts) in enumerate(plans):
        for at in range(0, rows, piece):
            full, scale = normalize(arrays[raw][pl.ds(at, piece), :])
            dnorm = arrays[base][pl.ds(start * rows + at, piece), :]
            for a, i in parts:
                dnorm = dnorm + decode(arrays[a], i * (rows + AUX), rows, at, piece)
            here = pl.ds(at, piece)
            mean = jnp.mean(dnorm * full, axis=-1, keepdims=True)
            buffers[k][here, :] = scale * (dnorm - full * mean)
            send(buffers[k].at[here], outs[k].at[here])
        if k == 0:
            values = [t[...] for t in terms] + [decode_loss(arrays[a]) for a in carried]
            loss_vmem[...] = jnp.sum(sum(values), keepdims=True) / (pairs * pairs)
            send(loss_vmem, outs[2])
    for copy in copies:
        copy.wait()


def combine(bits):
    masks = [0]
    for bit in bits:
        masks += [m ^ bit for m in masks]
    return masks


def on_device(core, bits_data, bits_param, sizes, data, param, region, partner, gain, shift):
    rows, width = data.shape
    msg = rows + AUX
    devices = sizes["row"] * sizes["col"]
    shape = jax.ShapeDtypeStruct

    def swap(x, mask):
        return lax.ppermute(x, ("row", "col"), [(i, i ^ mask) for i in range(devices)])

    param_msg, raw_data, side = call(
        pack_kernel,
        [shape((msg, width), BF16), shape((rows, width), BF16), shape((AUX, width), BF16)],
        [pl.BlockSpec(memory_space=pltpu.HBM)] * 4,
        [
            pltpu.VMEM((rows, width), BF16),
            pltpu.VMEM((1, rows), jnp.int32),
            pltpu.VMEM((1, rows), jnp.int32),
            pltpu.VMEM((AUX, width), F32),
            pltpu.SemaphoreType.DMA((4,)),
        ],
    )(data, param, region.reshape(1, rows), partner.reshape(1, rows))
    (data_msg,) = call(pack_data_kernel, [shape((msg, width), BF16)], [VMEM] * 2)(raw_data, side)
    held_p, masks_p = [param_msg], [0]
    held_d = [data_msg]
    for k in range(max(len(bits_data), len(bits_param))):
        if k < len(bits_param):
            held_p += [swap(x, bits_param[k]) for x in held_p]
            masks_p += [m ^ bits_param[k] for m in masks_p]
        if k < len(bits_data):
            held_d += [swap(x, bits_data[k]) for x in held_d]
    n_own, n_param = len(held_d), len(held_p)
    other_d = [swap(x, core) for x in held_d]
    columns = sizes["col"]
    coef = (gain, shift)
    me = lax.axis_index("row") * columns + lax.axis_index("col")
    both = jnp.stack([gain[0] / width, shift[0]])
    where = lambda g: (jnp.stack([(me ^ masks_p[i]) * rows for i in g]).astype(jnp.int32), both)
    n = n_own
    cols = n * rows
    late = [i for i in range(n_param) if i == n_param - 1]
    early = [i for i in range(n_param) if i not in late and not i & 1]
    middle = [i for i in range(n_param) if i not in late and i & 1]
    order = early + middle
    pick = lambda group: [masks_p[i] for i in group]
    data0, side0, acc0, loss = call(
        functools.partial(early_kernel, rows, n, pick(early), columns),
        [
            shape((cols, width), BF16),
            shape((8, cols), F32),
            shape((cols + len(early) * rows, width), F32),
            shape((8, 128), F32),
        ],
        [VMEM] * (n + len(early)) + [SMEM] * 2,
    )(*held_d[0::2], *other_d[0::2], *[held_p[i] for i in early], *where(early))
    data1, side1, acc0, acc1, parts, loss = call(
        functools.partial(middle_kernel, rows, n, len(early), pick(order), columns),
        [
            shape((cols, width), BF16),
            shape((8, cols), F32),
            shape((cols, width), F32),
            shape((cols, width), F32),
            shape((len(order) * rows, width), F32),
            shape((8, 128), F32),
        ],
        [VMEM] * (n + len(order) + 4) + [SMEM] * 2,
    )(
        *held_d[1::2], *other_d[1::2], *[held_p[i] for i in order], data0, side0, acc0, loss, *coef
    )
    top = n_param // 2
    ready = [k for k, i in enumerate(order) if i >= top]
    sent = [order[k] for k in ready] + late
    keep_d, low_d, top_d, loss, *send_p = call(
        functools.partial(late_kernel, rows, n, pick(late), columns, ready),
        [
            shape((n * rows, width), F32),
            *[shape((n // 2 * msg, width), I16)] * 2,
            shape((8, 128), F32),
            *[shape((msg, width), I16)] * len(sent),
        ],
        [VMEM] * (len(late) + 8) + [SMEM] * 2,
    )(
        *[held_p[i] for i in late],
        data0, side0, acc0, data1, side1, acc1, parts, loss, *coef,
    )
    columns = sizes["col"]
    inner = [b for b in bits_data + bits_param if b < columns]
    outer = [b for b in bits_data + bits_param if b >= columns]
    rounds = [inner, outer]
    got_top, got_low = swap(top_d, core), swap(low_d, core)
    terms, carriers = [loss], [got_top]

    def emit(items, step, with_loss):
        nonlocal terms, carriers
        arrays = []

        def slot(x):
            for i, y in enumerate(arrays):
                if x is y:
                    return i
            arrays.append(x)
            return len(arrays) - 1

        plan = [(slot(b), at, [(slot(x), i) for x, i in parts]) for b, at, parts in items]
        carried, outs = None, [shape((msg, width), I16)] * len(items)
        n_arrays = len(arrays)
        if with_loss and rounds:
            carried = [slot(x) for x in carriers]
            n_arrays = len(arrays)
            outs.append(shape((8, 128), F32))
            arrays = arrays + terms
        msgs = call(
            functools.partial(emit_kernel, rows, plan, n_arrays, carried),
            outs,
            [VMEM] * len(arrays),
        )(*arrays)
        got = [swap(x, step) for x in msgs[: len(items)]]
        if carried is not None:
            bits = rounds.pop(0)
            terms = [msgs[-1]] + [swap(msgs[-1], m) for m in combine(bits)[1:] if m != step]
            carriers = got[-1:] if step in bits else []
        return got

    half = n_own // 2
    items_d = [(keep_d, i, [(got_top if i >= half else got_low, i % half)]) for i in range(n_own)]
    items_p = [(parts, order.index(i), []) for i in range(top)]
    got = {i: swap(x, bits_param[-1]) for i, x in zip(sent, send_p)}
    for i in range(top):
        items_p[i][2].append((got[i + top], 0))
    left_d, left_p = bits_data[::-1], bits_param[-2::-1]
    while left_d or left_p:
        for items, left in ((items_d, left_d), (items_p, left_p)):
            if left:
                step, half = left.pop(0), len(items) // 2
                for i, x in enumerate(emit(items[half:], step, items is items_d)):
                    items[i][2].append((x, 0))
                del items[half:]
    arrays = []

    def slot(x):
        places = [i for i, y in enumerate(arrays) if y is x]
        if not places:
            arrays.append(x)
        return places[0] if places else len(arrays) - 1

    plans = [
        (slot(raw), slot(item[0]), item[1], [(slot(x), i) for x, i in item[2]])
        for raw, item in ((param, items_p[0]), (data, items_d[0]))
    ]
    carried = [slot(x) for x in carriers]
    grad_param, grad_data, loss = call(
        functools.partial(finish_kernel, rows, plans, len(arrays), carried, rows * devices),
        [shape((rows, width), F32)] * 2 + [shape((1, 1), F32)],
        [VMEM] * (len(arrays) + len(terms)),
        [
            *[pltpu.VMEM((rows, width), F32)] * 2,
            pltpu.VMEM((1, 1), F32),
            pltpu.SemaphoreType.DMA((7,)),
        ],
        to=pltpu.HBM,
    )(*arrays, *terms)
    return loss.reshape(1), grad_data, grad_param


def solution(mesh):
    sizes = dict(mesh.shape)
    columns = sizes["col"]
    col_bits = [1 << k for k in range(columns.bit_length() - 1)]
    row_bits = [columns << k for k in range(sizes["row"].bit_length() - 1)]
    core, rest = col_bits[0], col_bits[1:]
    odd = len(row_bits) & 1
    bits_data = row_bits[0::2] + rest[odd::2]
    bits_param = row_bits[1::2] + rest[1 - odd :: 2]
    split = P(("row", "col"))
    rows = P(("row", "col"), None)
    return jax.shard_map(
        functools.partial(on_device, core, bits_data, bits_param, sizes),
        mesh=mesh,
        in_specs=(rows, rows, split, split, P(), P()),
        out_specs=(P(), rows, rows),
        check_vma=False,
    )
```

```python
import functools

import jax
import jax.numpy as jnp
from jax import lax
from jax.experimental import pallas as pl
from jax.experimental.pallas import tpu as pltpu
from jax.sharding import PartitionSpec as P

AUX = 16
SUB = 8
FULL = 32000.0
LIMB = 16384.0
LOG2E = 1.4426950408889634
LN2 = 0.6931471805599453
VMEM = pl.BlockSpec(memory_space=pltpu.VMEM)
SMEM = pl.BlockSpec(memory_space=pltpu.SMEM)
F32 = jnp.float32
BF16 = jnp.bfloat16
I16 = jnp.int16


def call(body, out_shape, in_specs, scratch=(), aliases=None, vmem=16 * 2**20, to=pltpu.VMEM):
    inner = pl.pallas_call(
        body,
        out_shape=jax.tree.map(lambda s: to(s.shape, s.dtype), out_shape),
        in_specs=in_specs,
        input_output_aliases=aliases or {},
        cost_estimate=pl.CostEstimate(flops=1, bytes_accessed=1, transcendentals=0),
        out_specs=jax.tree.map(lambda _: pl.BlockSpec(memory_space=to), out_shape),
        scratch_shapes=list(scratch),
        compiler_params=pltpu.CompilerParams(vmem_limit_bytes=vmem),
    )

    def run(*args):
        args = [
            x if s is SMEM else pltpu.with_memory_space_constraint(x, s.memory_space)
            for x, s in zip(args, in_specs)
        ]
        return inner(*args)

    return run


def normalize(embed):
    full = embed.astype(F32)
    scale = lax.rsqrt(jnp.mean(full * full, axis=-1, keepdims=True) + 1e-06)
    return full * scale, scale


def pack_kernel(data_hbm, param_hbm, region_hbm, partner_hbm, param_msg, data, side, *scratch):
    param, region, partner, aux, sems = scratch
    rows = data.shape[0]
    pairs = ((param_hbm, param), (region_hbm, region), (partner_hbm, partner), (data_hbm, data))
    copies = [pltpu.make_async_copy(a, b, sems.at[i]) for i, (a, b) in enumerate(pairs)]
    for copy in copies:
        copy.start()
    aux[...] = jnp.zeros_like(aux)
    for copy in copies:
        copy.wait()
    index = partner[...]
    aux[0:1, 0:rows] = region[...].astype(F32)
    aux[1:2, 0:rows] = (index >> 8).astype(F32)
    aux[2:3, 0:rows] = (index & 255).astype(F32)
    side[...] = aux[...].astype(BF16)
    param_msg[pl.ds(rows, AUX), :] = side[...]
    param_msg[pl.ds(0, rows), :] = normalize(param[...])[0].astype(BF16)


def pack_data_kernel(data, side, data_msg):
    rows = data.shape[0]
    data_msg[pl.ds(rows, AUX), :] = side[...]
    data_msg[pl.ds(0, rows), :] = normalize(data[...])[0].astype(BF16)


def encode(value, ref, start, loss=None):
    rows, width = value.shape
    parts = value.reshape(rows // SUB, SUB, width)
    top = jnp.max(jnp.abs(parts), axis=0)
    power = jnp.ceil(jnp.log2(jnp.maximum(top, 1e-30)) * 256.0)
    unit = jnp.exp2(power * (-1.0 / 256.0)) * FULL
    coded = ((parts * unit[None] + 32768.5).astype(jnp.int32) - 32768).astype(I16)
    ref[pl.ds(start, rows), :] = coded.reshape(rows, width)
    below = jnp.zeros_like(power)
    if loss is not None:
        exponent = jnp.ceil(jnp.log2(jnp.maximum(loss, 1e-30)))
        mantissa = loss * jnp.exp2(-exponent) * LIMB
        high = jnp.floor(mantissa)
        low = jnp.floor((mantissa - high) * LIMB)
        rest = jnp.zeros((SUB, width - 3 * loss.shape[1]), F32)
        below = jnp.concatenate([exponent, high, low, rest], axis=1)
    aux = jnp.concatenate([power, below], axis=0)
    ref[pl.ds(start + rows, AUX), :] = aux.astype(jnp.int32).astype(I16)


def decode(ref, start, rows, at=0, piece=None):
    piece, width = piece or rows, ref.shape[-1]
    coded = ref[pl.ds(start + at, piece), :].astype(F32).reshape(piece // SUB, SUB, width)
    power = ref[pl.ds(start + rows, AUX), :].astype(F32)[:SUB]
    unit = jnp.exp2(power * (1.0 / 256.0)) * (1.0 / FULL)
    return (coded * unit[None]).reshape(piece, width)


def decode_loss(ref):
    aux = pl.ds(ref.shape[0] - AUX, AUX)
    exponent, high, low = jnp.split(ref[aux, :].astype(F32)[SUB:, :384], 3, axis=1)
    return (high + low * (1.0 / LIMB)) * (1.0 / LIMB) * jnp.exp2(exponent)


def log1p(t):
    u = 1.0 + t
    small = t * (1.0 - t * (0.5 - t * (1.0 / 3.0)))
    return jnp.where(t < 0.01, small, jnp.log(u))


LAST = (((1,), (1,)), ((), ()))
FIRST = (((0,), (0,)), ((), ()))


def load_data(msgs, data, side, rows):
    for i, msg in enumerate(msgs):
        at = pl.ds(i * rows, rows)
        data[at, :] = msg[pl.ds(0, rows), :]
        aux = msg[pl.ds(rows, AUX), :].astype(F32)[:, :rows]
        side[0:1, at] = aux[0:1]
        side[1:2, at] = aux[1:2] * 256.0 + aux[2:3]


def side_columns(msg, base, rows):
    square = (rows + 127) // 128 * 128
    lane = lax.broadcasted_iota(jnp.int32, (rows, square), 1)
    eye = (lax.broadcasted_iota(jnp.int32, (rows, square), 0) == lane).astype(F32).astype(BF16)
    aux = msg[pl.ds(rows, AUX), :][:, :square]
    region = lax.dot_general(eye, aux, LAST, preferred_element_type=F32)[:, 0:1]
    place = lax.broadcasted_iota(jnp.int32, (rows, 1), 0) + base
    return region, place.astype(F32)


def tile(block, columns, data, side, coef, shift):
    region_col, index_col = columns
    rows, cols = block.shape[0], data.shape[0]
    dots = lax.dot_general(block, data[...], LAST, preferred_element_type=F32)
    positive = index_col == side[1:2, :]
    keep = jnp.logical_or(positive, region_col != side[0:1, :])
    x = dots * (coef * LOG2E) + shift * LOG2E
    x = jnp.where(positive, -x, x)
    t = jnp.where(keep, jnp.exp2(x), 0.0)
    slope = t / (1.0 + t)
    grad = (jnp.where(positive, -slope, slope) * coef).astype(BF16)
    q = t.reshape(4, rows // 4, cols)
    t01 = q[0] + q[1] * (1.0 + q[0])
    t23 = q[2] + q[3] * (1.0 + q[2])
    terms = log1p(t01 + t23 * (1.0 + t01)).reshape(rows // 32, 8, cols)
    terms = jnp.sum(terms, axis=0)
    loss = terms[:, 0:128]
    for k in range(128, cols, 128):
        loss = loss + terms[:, k : k + 128]
    return grad, loss


def scalars(refs, masks, columns_n, rows, width):
    me = lax.axis_index("row") * columns_n + lax.axis_index("col")
    return [(me ^ m) * rows for m in masks], (refs[0][0] * (1.0 / width), refs[1][0])


def tables(refs, masks, columns_n, rows, width):
    return [refs[0][i] for i in range(len(masks))], (refs[1][0], refs[1][1])


def early_kernel(rows, n, masks, columns_n, *refs):
    p_n = len(masks)
    msgs, params = refs[:n], refs[n : n + p_n]
    width = msgs[0].shape[1]
    base, coef = tables(refs[n + p_n : n + p_n + 2], masks, columns_n, rows, width)
    data, side, acc, loss_out = refs[n + p_n + 2 :]
    cols = n * rows
    load_data(msgs, data, side, rows)
    loss = jnp.zeros((8, 128), F32)
    for s in range(p_n):
        block = params[s][pl.ds(0, rows), :]
        columns = side_columns(params[s], base[s], rows)
        grad, term = tile(block, columns, data, side, coef[0], coef[1])
        loss = loss + term
        at = pl.ds(cols + s * rows, rows)
        acc[at, :] = jnp.dot(grad, data[...], preferred_element_type=F32)
        d_part = lax.dot_general(grad, block, FIRST, preferred_element_type=F32)
        acc[pl.ds(0, cols), :] = d_part if s == 0 else acc[pl.ds(0, cols), :] + d_part
    loss_out[...] = loss


def middle_kernel(rows, n, p_n, masks, columns_n, *refs):
    m_n = len(masks) - p_n
    msgs, params = refs[:n], refs[n : n + p_n + m_n]
    data0, side0, acc0, loss_in = refs[n + p_n + m_n : n + p_n + m_n + 4]
    width = msgs[0].shape[1]
    base, coef = scalars(refs[n + p_n + m_n + 4 : n + p_n + m_n + 6], masks, columns_n, rows, width)
    data, side, acc0_out, acc, parts, loss_out = refs[n + p_n + m_n + 6 :]
    cols = n * rows
    whole = pl.ds(0, cols)
    load_data(msgs, data, side, rows)
    loss = loss_in[...]
    for s in range(p_n + m_n):
        at = pl.ds(s * rows, rows)
        block = params[s][pl.ds(0, rows), :]
        columns = side_columns(params[s], base[s], rows)
        grad, term = tile(block, columns, data, side, coef[0], coef[1])
        loss = loss + term
        part = jnp.dot(grad, data[...], preferred_element_type=F32)
        d_part = lax.dot_general(grad, block, FIRST, preferred_element_type=F32)
        acc[...] = d_part if s == 0 else acc[...] + d_part
        if s < p_n:
            parts[at, :] = acc0[pl.ds(cols + s * rows, rows), :] + part
            continue
        grad, term = tile(block, columns, data0, side0, coef[0], coef[1])
        loss = loss + term
        parts[at, :] = part + jnp.dot(grad, data0[...], preferred_element_type=F32)
        d_part = lax.dot_general(grad, block, FIRST, preferred_element_type=F32)
        acc0_out[...] = (acc0[whole, :] if s == p_n else acc0_out[...]) + d_part
    if m_n == 0:
        acc0_out[...] = acc0[whole, :]
    loss_out[...] = loss


def late_kernel(rows, n, masks, columns_n, ready, *refs):
    l_n = len(masks)
    params = refs[:l_n]
    data0, side0, acc0, data1, side1, acc1, parts, loss_in = refs[l_n : l_n + 8]
    width = params[0].shape[1]
    base, coef = scalars(refs[l_n + 8 : l_n + 10], masks, columns_n, rows, width)
    outs = refs[l_n + 10 :]
    keep_d, low_d, top_d, loss_out = outs[:4]
    send_p = outs[4:]
    loss = loss_in[...]
    half = n // 2
    for k, s in enumerate(ready):
        encode(parts[pl.ds(s * rows, rows), :], send_p[k], 0)
    for s in range(l_n):
        block = params[s][pl.ds(0, rows), :]
        columns = side_columns(params[s], base[s], rows)
        total = None
        for h, (data, side, acc) in enumerate(((data0, side0, acc0), (data1, side1, acc1))):
            grad, term = tile(block, columns, data, side, coef[0], coef[1])
            loss = loss + term
            part = jnp.dot(grad, data[...], preferred_element_type=F32)
            total = part if total is None else total + part
            d_part = acc[...] + lax.dot_general(grad, block, FIRST, preferred_element_type=F32)
            if s < l_n - 1:
                acc[...] = d_part
                continue
            for i in range(half):
                place = 2 * i + h
                keep_d[pl.ds(place * rows, rows), :] = d_part[i * rows : (i + 1) * rows]
                send_d = top_d if place >= half else low_d
                at = half + i
                part = d_part[at * rows : (at + 1) * rows]
                with_loss = loss if place == n - 1 else None
                encode(part, send_d, place % half * (rows + AUX), with_loss)
        encode(total, send_p[len(ready) + s], 0)
    loss_out[...] = loss


def emit_kernel(rows, plan, n_arrays, carried, *refs):
    arrays, terms, outs = refs[:n_arrays], refs[n_arrays:], None
    loss = None
    if carried is None:
        outs = terms
    else:
        terms, outs = terms[: -len(plan) - 1], terms[-len(plan) - 1 :]
        loss = sum([t[...] for t in terms] + [decode_loss(arrays[a]) for a in carried])
        outs[-1][...] = loss
    for out, (b, start, parts) in zip(outs, plan):
        total = arrays[b][pl.ds(start * rows, rows), :]
        for a, i in parts:
            total = total + decode(arrays[a], i * (rows + AUX), rows)
        encode(total, out, 0, loss)


def backward(refs, plan, rows, at, piece):
    raw, base, start, parts = plan
    full, scale = normalize(refs[raw][pl.ds(at, piece), :])
    dnorm = refs[base][pl.ds(start * rows + at, piece), :]
    for a, i in parts:
        dnorm = dnorm + decode(refs[a], i * (rows + AUX), rows, at, piece)
    return scale * (dnorm - full * jnp.mean(dnorm * full, axis=-1, keepdims=True))


def param_kernel(rows, plan, *refs):
    refs[-1][...] = backward(refs, plan, rows, 0, rows)


def finish_kernel(rows, plan, n_arrays, carried, pairs, ready, *refs):
    arrays, terms, outs = refs[:n_arrays], refs[n_arrays:-6], refs[-6:-3]
    buffer, loss_vmem, sems = refs[-3:]
    copies = []

    def send(a, b):
        copies.append(pltpu.make_async_copy(a, b, sems.at[len(copies)]))
        copies[-1].start()

    send(ready, outs[0])
    values = [t[...] for t in terms] + [decode_loss(arrays[a]) for a in carried]
    loss_vmem[...] = jnp.sum(sum(values), keepdims=True) / (pairs * pairs)
    send(loss_vmem, outs[2])
    piece = rows // 3 if rows % (3 * AUX) == 0 else rows
    for at in range(0, rows, piece):
        here = pl.ds(at, piece)
        buffer[here, :] = backward(arrays, plan, rows, at, piece)
        send(buffer.at[here], outs[1].at[here])
    for copy in copies:
        copy.wait()


def combine(bits):
    masks = [0]
    for bit in bits:
        masks += [m ^ bit for m in masks]
    return masks


def on_device(core, bits_data, bits_param, sizes, data, param, region, partner, gain, shift):
    rows, width = data.shape
    msg = rows + AUX
    devices = sizes["row"] * sizes["col"]
    shape = jax.ShapeDtypeStruct

    def swap(x, mask):
        return lax.ppermute(x, ("row", "col"), [(i, i ^ mask) for i in range(devices)])

    param_msg, raw_data, side = call(
        pack_kernel,
        [shape((msg, width), BF16), shape((rows, width), BF16), shape((AUX, width), BF16)],
        [pl.BlockSpec(memory_space=pltpu.HBM)] * 4,
        [
            pltpu.VMEM((rows, width), BF16),
            pltpu.VMEM((1, rows), jnp.int32),
            pltpu.VMEM((1, rows), jnp.int32),
            pltpu.VMEM((AUX, width), F32),
            pltpu.SemaphoreType.DMA((4,)),
        ],
    )(data, param, region.reshape(1, rows), partner.reshape(1, rows))
    (data_msg,) = call(pack_data_kernel, [shape((msg, width), BF16)], [VMEM] * 2)(raw_data, side)
    held_p, masks_p = [param_msg], [0]
    held_d = [data_msg]
    for k in range(max(len(bits_data), len(bits_param))):
        if k < len(bits_param):
            held_p += [swap(x, bits_param[k]) for x in held_p]
            masks_p += [m ^ bits_param[k] for m in masks_p]
        if k < len(bits_data):
            held_d += [swap(x, bits_data[k]) for x in held_d]
    n_own, n_param = len(held_d), len(held_p)
    other_d = [swap(x, core) for x in held_d]
    columns = sizes["col"]
    coef = (gain, shift)
    me = lax.axis_index("row") * columns + lax.axis_index("col")
    both = jnp.stack([gain[0] / width, shift[0]])
    where = lambda g: (jnp.stack([(me ^ masks_p[i]) * rows for i in g]).astype(jnp.int32), both)
    n = n_own
    cols = n * rows
    late = [i for i in range(n_param) if i == n_param - 1]
    early = [i for i in range(n_param) if i not in late and not i & 1]
    middle = [i for i in range(n_param) if i not in late and i & 1]
    order = early + middle
    pick = lambda group: [masks_p[i] for i in group]
    data0, side0, acc0, loss = call(
        functools.partial(early_kernel, rows, n, pick(early), columns),
        [
            shape((cols, width), BF16),
            shape((8, cols), F32),
            shape((cols + len(early) * rows, width), F32),
            shape((8, 128), F32),
        ],
        [VMEM] * (n + len(early)) + [SMEM] * 2,
    )(*held_d[0::2], *other_d[0::2], *[held_p[i] for i in early], *where(early))
    data1, side1, acc0, acc1, parts, loss = call(
        functools.partial(middle_kernel, rows, n, len(early), pick(order), columns),
        [
            shape((cols, width), BF16),
            shape((8, cols), F32),
            shape((cols, width), F32),
            shape((cols, width), F32),
            shape((len(order) * rows, width), F32),
            shape((8, 128), F32),
        ],
        [VMEM] * (n + len(order) + 4) + [SMEM] * 2,
    )(
        *held_d[1::2], *other_d[1::2], *[held_p[i] for i in order], data0, side0, acc0, loss, *coef
    )
    top = n_param // 2
    ready = [k for k, i in enumerate(order) if i >= top]
    sent = [order[k] for k in ready] + late
    keep_d, low_d, top_d, loss, *send_p = call(
        functools.partial(late_kernel, rows, n, pick(late), columns, ready),
        [
            shape((n * rows, width), F32),
            *[shape((n // 2 * msg, width), I16)] * 2,
            shape((8, 128), F32),
            *[shape((msg, width), I16)] * len(sent),
        ],
        [VMEM] * (len(late) + 8) + [SMEM] * 2,
    )(
        *[held_p[i] for i in late],
        data0, side0, acc0, data1, side1, acc1, parts, loss, *coef,
    )
    columns = sizes["col"]
    inner = [b for b in bits_data + bits_param if b < columns]
    outer = [b for b in bits_data + bits_param if b >= columns]
    rounds = [inner, outer]
    got_top, got_low = swap(top_d, core), swap(low_d, core)
    terms, carriers = [loss], [got_top]

    def emit(items, step, with_loss):
        nonlocal terms, carriers
        arrays = []

        def slot(x):
            for i, y in enumerate(arrays):
                if x is y:
                    return i
            arrays.append(x)
            return len(arrays) - 1

        plan = [(slot(b), at, [(slot(x), i) for x, i in parts]) for b, at, parts in items]
        carried, outs = None, [shape((msg, width), I16)] * len(items)
        n_arrays = len(arrays)
        if with_loss and rounds:
            carried = [slot(x) for x in carriers]
            n_arrays = len(arrays)
            outs.append(shape((8, 128), F32))
            arrays = arrays + terms
        msgs = call(
            functools.partial(emit_kernel, rows, plan, n_arrays, carried),
            outs,
            [VMEM] * len(arrays),
        )(*arrays)
        got = [swap(x, step) for x in msgs[: len(items)]]
        if carried is not None:
            bits = rounds.pop(0)
            terms = [msgs[-1]] + [swap(msgs[-1], m) for m in combine(bits)[1:] if m != step]
            carriers = got[-1:] if step in bits else []
        return got

    half = n_own // 2
    items_d = [(keep_d, i, [(got_top if i >= half else got_low, i % half)]) for i in range(n_own)]
    items_p = [(parts, order.index(i), []) for i in range(top)]
    got = {i: swap(x, bits_param[-1]) for i, x in zip(sent, send_p)}
    for i in range(top):
        items_p[i][2].append((got[i + top], 0))
    left_d, left_p = bits_data[::-1], bits_param[-2::-1]
    while left_d or left_p:
        for items, left in ((items_d, left_d), (items_p, left_p)):
            if left:
                step, half = left.pop(0), len(items) // 2
                for i, x in enumerate(emit(items[half:], step, items is items_d)):
                    items[i][2].append((x, 0))
                del items[half:]
    def plan_of(raw, item, more=()):
        arrays = []

        def slot(x):
            places = [i for i, y in enumerate(arrays) if y is x]
            if not places:
                arrays.append(x)
            return places[0] if places else len(arrays) - 1

        plan = (slot(raw), slot(item[0]), item[1], [(slot(x), i) for x, i in item[2]])
        return plan, [slot(x) for x in more], arrays

    plan, _, arrays = plan_of(param, items_p[0])
    (ready_p,) = call(
        functools.partial(param_kernel, rows, plan), [shape((rows, width), F32)], [VMEM] * len(arrays)
    )(*arrays)
    plan, carried, arrays = plan_of(data, items_d[0], carriers)
    grad_param, grad_data, loss = call(
        functools.partial(finish_kernel, rows, plan, len(arrays), carried, rows * devices),
        [shape((rows, width), F32)] * 2 + [shape((1, 1), F32)],
        [VMEM] * (1 + len(arrays) + len(terms)),
        [
            pltpu.VMEM((rows, width), F32),
            pltpu.VMEM((1, 1), F32),
            pltpu.SemaphoreType.DMA((5,)),
        ],
        to=pltpu.HBM,
    )(ready_p, *arrays, *terms)
    return loss.reshape(1), grad_data, grad_param


def solution(mesh):
    sizes = dict(mesh.shape)
    columns = sizes["col"]
    col_bits = [1 << k for k in range(columns.bit_length() - 1)]
    row_bits = [columns << k for k in range(sizes["row"].bit_length() - 1)]
    core, rest = col_bits[0], col_bits[1:]
    odd = len(row_bits) & 1
    bits_data = row_bits[0::2] + rest[odd::2]
    bits_param = row_bits[1::2] + rest[1 - odd :: 2]
    split = P(("row", "col"))
    rows = P(("row", "col"), None)
    return jax.shard_map(
        functools.partial(on_device, core, bits_data, bits_param, sizes),
        mesh=mesh,
        in_specs=(rows, rows, split, split, P(), P()),
        out_specs=(P(), rows, rows),
        check_vma=False,
    )
```
